256 devices in a mesh: member: 4 (over z_lo, core), tile: 64 (over y, x, z_hi).
Axes of the slice: x: 4, y: 4, z: 8 (z_hi: 4, z_lo: 2; z = z_hi * 2 + z_lo), core: 2. Of those that a mesh axis runs over, the one named last changes fastest.
Arguments:
- member_predictions: bfloat16 [4, 80, 3072, 1536], P(None, 'member', 'tile'), may hold values from -5 to 13
- meridional_operator: float32 [384, 128], replicated, may hold values from -0.3125 to 0.3125
- zonal_operator: float32 [1024, 48], P('tile'), may hold values from -0.875 to 0.875
Outputs:
- coarse_anomalies: float32 [4, 80, 512, 1024], P(None, None, 'tile', 'member')
The draws below stay inside these ranges and needn't reach their ends.
All inputs are finite; a program needn't handle non-finite values.
Results may differ from the reference program's by a relative error of at most 0.0003.
Values sent between devices are 32-bit elements; how exact they have to be, the bound alone decides.
No kernel may reach another device: no remote copies, remote signals or barrier semaphores. Data moves between devices by JAX's collectives and lax.ppermute only.
A program may use at most 128 MiB of HBM per device.

```python
import math
import jax
import jax.numpy as jnp
from jax import lax

M = 80
LEV = 4
LON_DEV = 48
NY = 1536
LB = 384
LBC = 128
NX = 3072
NXC = 1024


def draw_member_predictions(key, part):
    key = jax.random.fold_in(key, 11)
    key_back, key_pert = jax.random.split(key, 2)
    background = jax.random.uniform(key_back, (LEV, 1, NX, NY), jnp.float32, 2.0, 6.0)
    perturbation = jnp.clip(jax.random.normal(key_pert, (LEV, M, NX, NY), jnp.float32), -5.0, 5.0)
    return (background + perturbation).astype(jnp.bfloat16)


def shard_levels(stream_key, dims, pieces, low, high):
    loudness, own = 1.0, jax.random.fold_in(stream_key, 6)
    for axis_at, shards_of in pieces:
        heights = jnp.exp(jax.random.uniform(jax.random.fold_in(own, axis_at), (shards_of,), jnp.float32, low / len(pieces), high / len(pieces)))
        loudness = loudness * jnp.repeat(heights, dims[axis_at] // shards_of).reshape([-1 if axis == axis_at else 1 for axis in range(len(dims))])
    return loudness


def centred(stream_key, dims, scale, reach, cuts=(), kind=jnp.bfloat16):
    array = jax.random.normal(stream_key, dims, jnp.float32) * scale
    if len(cuts) > 0:
        array = shard_levels(stream_key, dims, cuts, -0.22, 0.18) * array
    return jnp.clip(array, min=-reach, max=reach).astype(kind)


def setup_inputs(seed: int = 0) -> dict:
    splits = jax.random.split(jax.random.key(seed), 4)
    member_predictions = draw_member_predictions(jax.random.fold_in(splits[3], 71), 0)
    meridional_operator = centred(splits[1], (LB, LBC), LB ** -0.5, 0.3125, (), jnp.float32)
    zonal_operator = centred(splits[2], (NXC, LON_DEV), LON_DEV ** -0.5, 0.875, ((0, 64),), jnp.float32)
    return dict(member_predictions=member_predictions, meridional_operator=meridional_operator, zonal_operator=zonal_operator)


def restrict_one(field, meridional_operator, zonal_operator):
    latitude_bands = field.reshape(NX, NY // LB, LB)
    across = jnp.einsum('xbj,jk->xbk', latitude_bands, meridional_operator, precision=lax.Precision.HIGHEST)
    across = across.reshape(NX // LON_DEV, LON_DEV, NY // 3)
    lon_tiled = zonal_operator.reshape(NX // LON_DEV, LON_DEV // 3, LON_DEV)
    result = jnp.einsum('tcx,txi->itc', lon_tiled, across, precision=lax.Precision.HIGHEST)
    return result.reshape(NY // 3, NX // 3)

def one_layer_slice(stacked_layer_states, meridional_operator, zonal_operator):

    def running_total(total, member_field):
        return (total + member_field.astype(jnp.float32), None)
    total, _ = lax.scan(running_total, jnp.zeros((NX, NY), jnp.float32), stacked_layer_states)
    ens_mean = total / M
    scale = 1.0 / math.sqrt(M - 1)

    def per_member(member_field):
        anomaly = (member_field.astype(jnp.float32) - ens_mean) * scale
        return restrict_one(anomaly, meridional_operator, zonal_operator)
    return lax.map(per_member, stacked_layer_states)

def reference(member_predictions, meridional_operator, zonal_operator):
    return lax.map(lambda stacked_layer_states: one_layer_slice(stacked_layer_states, meridional_operator, zonal_operator), member_predictions)
```

```python
import functools
import math

import jax
import jax.numpy as jnp
from jax import lax
from jax.experimental import pallas as pl
from jax.experimental.pallas import tpu as pltpu
from jax.sharding import Mesh
from jax.sharding import PartitionSpec as P

M = 80
AX = ("zlo", "core", "y", "x", "zhi")
PAIRS = 8
ROWS = 384
CUT, GROUPS = 4, 10
ANY = pl.BlockSpec(memory_space=pl.ANY)


def split2(v):
    hi = v.astype(jnp.bfloat16)
    return hi, (v - hi.astype(jnp.float32)).astype(jnp.bfloat16)


def restrict_kernel(first, count, x_ref, mer_ref, zon_ref, *rest):
    outs, (buf, mer_buf, zon_buf, stage, in_sems, op_sems, out_sems) = rest[:4], rest[4:]
    base = lax.axis_index("y")

    def load(g, j):
        rows = pl.ds((first + g) * ROWS, ROWS)
        lane = pl.multiple_of((base ^ j) * ROWS, 128)
        to = buf.at[g, :, pl.ds(j * ROWS, ROWS)]
        return pltpu.make_async_copy(x_ref.at[rows, pl.ds(lane, ROWS)], to, in_sems.at[g, j])

    def store(g, j):
        lanes = pl.ds(128 * g, 128)
        return pltpu.make_async_copy(stage.at[j, :, :, lanes], outs[j].at[:, :, lanes], out_sems.at[g, j])

    get_mer = pltpu.make_async_copy(mer_ref, mer_buf, op_sems.at[0])
    get_zon = pltpu.make_async_copy(zon_ref, zon_buf, op_sems.at[1])
    get_zon.start()
    get_mer.start()
    for g in range(count):
        for j in range(4):
            load(g, j).start()
    k = lax.broadcasted_iota(jnp.int32, (48, 192), 0)
    n = lax.broadcasted_iota(jnp.int32, (48, 192), 1)
    spread = jnp.where(lax.rem(n, 48) == k, 1.0, 0.0).astype(jnp.bfloat16)
    row = lax.broadcasted_iota(jnp.int32, (64, 192), 0)
    col = lax.broadcasted_iota(jnp.int32, (64, 192), 1) - 48 * lax.shift_right_logical(row, 4)
    keep = (col >= 0) & (col < 48)
    get_zon.wait()
    tiles = []
    for part in split2(zon_buf[...]):
        wide = jnp.dot(part, spread, preferred_element_type=jnp.float32)
        wide = jnp.concatenate([wide] * 4, axis=0)
        tiles.append(jnp.where(keep, wide, 0.0).astype(jnp.bfloat16))
    zon = jnp.concatenate(tiles, axis=0)
    get_mer.wait()
    mer = jnp.concatenate(split2(mer_buf[...]), axis=1)

    for g in range(count):
        for j in range(4):
            load(g, j).wait()
        w = []
        for q in range(2):
            t = jnp.dot(zon, buf[g, 192 * q : 192 * q + 192], preferred_element_type=jnp.float32)
            w.append(t[:64] + t[64:])
        w = jnp.concatenate(split2(jnp.concatenate(w, axis=0)), axis=0)
        for j in range(4):
            v = jnp.dot(w[:, j * ROWS : (j + 1) * ROWS], mer, preferred_element_type=jnp.float32)
            v = (v[128:, 128:] + v[128:, :128]) + v[:128, 128:] + v[:128, :128]
            stage[j, :, :, 128 * g : 128 * g + 128] = v.T.reshape(16, 8, 128)
            store(g, j).start()
    for g in range(count):
        for j in range(4):
            store(g, j).wait()


def restrict(x, mer, zon, first, count):
    lanes = count * 128
    return pl.pallas_call(
        functools.partial(restrict_kernel, first, count),
        out_shape=[jax.ShapeDtypeStruct((16, 8, lanes), jnp.float32)] * 4,
        in_specs=[ANY] * 3,
        out_specs=[ANY] * 4,
        scratch_shapes=[
            pltpu.VMEM((count, ROWS, 4 * ROWS), jnp.bfloat16),
            pltpu.VMEM(mer.shape, jnp.float32),
            pltpu.VMEM(zon.shape, jnp.float32),
            pltpu.VMEM((4, 16, 8, lanes), jnp.float32),
            pltpu.SemaphoreType.DMA((count, 4)),
            pltpu.SemaphoreType.DMA((2,)),
            pltpu.SemaphoreType.DMA((count, 4)),
        ],
        compiler_params=pltpu.CompilerParams(vmem_limit_bytes=56 * 2**20),
        cost_estimate=pl.CostEstimate(
            flops=count * 800_000_000, bytes_accessed=count * ROWS * ROWS * 16, transcendentals=0
        ),
        name=f"restrict_{first}",
    )(x, mer, zon)


def swap_groups(v):
    group = lax.shift_right_logical(lax.broadcasted_iota(jnp.int32, (8, 128), 1), 4)
    for d in (4, 2, 1):
        low = (group & d) == 0
        new = list(v)
        for i in range(8):
            if i & d:
                continue
            a, b = v[i], v[i + d]
            if d == 4:
                c = pltpu.roll(jnp.where(low, b, a), 64, 1)
                new[i], new[i + d] = jnp.where(low, a, c), jnp.where(low, c, b)
            else:
                new[i] = jnp.where(low, a, pltpu.roll(b, 16 * d, 1))
                new[i + d] = jnp.where(low, pltpu.roll(a, 128 - 16 * d, 1), b)
        v = new
    return v


def finish_kernel(levels, tiles1, tiles2, *refs):
    refs = list(refs)
    r1 = refs.pop(0)
    r2 = refs.pop(0) if tiles2 else None
    if tiles2:
        refs.pop(0)
    out, b1, b2, stage, in_sems, out_sems = refs
    y = lax.axis_index("y")
    wide1 = pl.ds(128 * tiles1[0], 128 * len(tiles1))

    def loads(h):
        rows = pl.ds(8 * h, 8)
        found = [pltpu.make_async_copy(r1.at[:, rows, :, wide1], b1.at[:, rows], in_sems.at[h, 0])]
        if tiles2:
            found.append(pltpu.make_async_copy(r2.at[:, rows], b2.at[:, rows], in_sems.at[h, 1]))
        return found

    def store(h, n):
        lanes = pl.ds(128 * h, 128)
        return pltpu.make_async_copy(stage.at[n, :, :, lanes], out.at[levels[n], :, :, lanes], out_sems.at[h, n])

    for h in range(2):
        for c in loads(h):
            c.start()
    scale = 1.0 / math.sqrt(M - 1)
    for h in range(2):
        for c in loads(h):
            c.wait()
        lanes = slice(128 * h, 128 * h + 128)

        def shuffle(k, sums):
            sums = list(sums)
            p = y ^ k
            for tile in (*tiles1, *tiles2):
                if tile < CUT:
                    at = 128 * (tile - tiles1[0])
                    v = [b1[k, 8 * h + i, :, at : at + 128] for i in range(8)]
                else:
                    at = 128 * (tile - CUT)
                    v = [b2[k, 8 * h + i, :, at : at + 128] for i in range(8)]
                v = swap_groups(v)
                for i in range(8):
                    level, m = divmod(8 * tile + i, 20)
                    if level in levels:
                        n = level - levels[0]
                        stage[n, p * 20 + m, :, lanes] = v[i]
                        sums[n] = sums[n] + v[i]
            return tuple(sums)

        zero = jnp.zeros((8, 128), jnp.float32)
        sums = lax.fori_loop(0, 4, shuffle, (zero,) * len(levels))
        for n in range(len(levels)):
            mean = sums[n] / M

            def centre(q, _):
                for m in range(20):
                    stage[n, q * 20 + m, :, lanes] = (stage[n, q * 20 + m, :, lanes] - mean) * scale
                return 0

            lax.fori_loop(0, 4, centre, 0)
            store(h, n).start()
    for h in range(2):
        for n in range(len(levels)):
            store(h, n).wait()


def finish(levels, r1, r2, earlier):
    first, last = 20 * levels[0] // PAIRS, (20 * levels[-1] + 19) // PAIRS
    tiles1 = tuple(range(first, min(last + 1, CUT)))
    tiles2 = tuple(range(CUT, last + 1))
    operands, aliases = [r1], {}
    if tiles2:
        operands, aliases = [r1, r2, earlier], {2: 0}
    return pl.pallas_call(
        functools.partial(finish_kernel, levels, tiles1, tiles2),
        out_shape=jax.ShapeDtypeStruct((4, M, 8, 256), jnp.float32),
        in_specs=[ANY] * len(operands),
        out_specs=ANY,
        input_output_aliases=aliases,
        scratch_shapes=[
            pltpu.VMEM((4, 16, 8, 128 * len(tiles1)), jnp.float32),
            pltpu.VMEM((4, 16, 8, 128 * max(1, len(tiles2))), jnp.float32),
            pltpu.VMEM((len(levels), M, 8, 256), jnp.float32),
            pltpu.SemaphoreType.DMA((2, 2)),
            pltpu.SemaphoreType.DMA((2, len(levels))),
        ],
        compiler_params=pltpu.CompilerParams(vmem_limit_bytes=16 * 2**20),
        cost_estimate=pl.CostEstimate(
            flops=len(levels) * 2_000_000, bytes_accessed=len(levels) * 1_300_000, transcendentals=0
        ),
        name=f"finish_{levels[0]}",
    )(*operands)


def swap_y(k):
    return [(a * 64 + y * 16 + b, a * 64 + (y ^ k) * 16 + b) for a in range(4) for y in range(4) for b in range(16)]


def planes():
    return [[(y ^ j) * 64 + y * 16 + b for j in range(4) for b in range(16)] for y in range(4)]


def along_y(parts):
    return jnp.concatenate([parts[0]] + [lax.ppermute(parts[k], AX, swap_y(k)) for k in (1, 2, 3)], axis=0)


def across_plane(v):
    return lax.all_to_all(v, AX, 0, 0, axis_index_groups=planes(), tiled=True).reshape(4, 16, 8, -1)


def body(member_predictions, meridional_operator, zonal_operator):
    x = member_predictions.reshape(-1, member_predictions.shape[-1])
    ops = (meridional_operator, zonal_operator)
    one = along_y(restrict(x, *ops, 0, CUT))
    two = restrict(x, *ops, CUT, GROUPS - CUT)
    one, *two = lax.optimization_barrier((one, *two))
    one, two = across_plane(one), across_plane(along_y(two))
    return finish((1, 2, 3), one, two, finish((0,), one, None, None))


def solution(mesh):
    fine = Mesh(mesh.devices.reshape(2, 2, 4, 4, 4), AX)
    member, tile = ("zlo", "core"), ("y", "x", "zhi")
    in_specs = (P(None, member, tile, None), P(), P(tile, None))
    out_specs = P(None, None, tile, member)
    return jax.shard_map(body, mesh=fine, in_specs=in_specs, out_specs=out_specs, check_vma=False)
```

```python
import functools
import math

import jax
import jax.numpy as jnp
from jax import lax
from jax.experimental import pallas as pl
from jax.experimental.pallas import tpu as pltpu
from jax.sharding import Mesh
from jax.sharding import PartitionSpec as P

M = 80
AX = ("zlo", "core", "y", "x", "zhi")
PAIRS = 8
ROWS = 384
CUT, GROUPS = 4, 10
ANY = pl.BlockSpec(memory_space=pl.ANY)


def split2(v):
    hi = v.astype(jnp.bfloat16)
    return hi, (v - hi.astype(jnp.float32)).astype(jnp.bfloat16)


def own_member():
    return 2 * lax.axis_index("zlo") + lax.axis_index("core")


def restrict_kernel(first, count, along_y, x_ref, mer_ref, zon_ref, *rest):
    outs, (buf, mid, mer_buf, zon_buf, stage, in_sems, op_sems, out_sems) = rest[:4], rest[4:]
    base = lax.axis_index("y")
    at_x, at_z = lax.axis_index("x"), lax.axis_index("zhi")

    def load(g, j):
        rows = pl.ds((first + g) * ROWS, ROWS)
        lane = pl.multiple_of((base ^ j) * ROWS, 128)
        to = buf.at[g, :, pl.ds(j * ROWS, ROWS)]
        return pltpu.make_async_copy(x_ref.at[rows, pl.ds(lane, ROWS)], to, in_sems.at[g, j])

    def store(j):
        return pltpu.make_async_copy(stage.at[j], outs[j], out_sems.at[j])

    get_mer = pltpu.make_async_copy(mer_ref, mer_buf, op_sems.at[0])
    get_zon = pltpu.make_async_copy(zon_ref, zon_buf, op_sems.at[1])
    get_zon.start()
    get_mer.start()
    for g in range(count):
        for j in range(4):
            load(g, j).start()
    k = lax.broadcasted_iota(jnp.int32, (48, 192), 0)
    n = lax.broadcasted_iota(jnp.int32, (48, 192), 1)
    spread = jnp.where(lax.rem(n, 48) == k, 1.0, 0.0).astype(jnp.bfloat16)
    row = lax.broadcasted_iota(jnp.int32, (64, 192), 0)
    col = lax.broadcasted_iota(jnp.int32, (64, 192), 1) - 48 * lax.shift_right_logical(row, 4)
    keep = (col >= 0) & (col < 48)
    get_zon.wait()
    tiles = []
    for part in split2(zon_buf[...]):
        wide = jnp.dot(part, spread, preferred_element_type=jnp.float32)
        wide = jnp.concatenate([wide] * 4, axis=0)
        tiles.append(jnp.where(keep, wide, 0.0).astype(jnp.bfloat16))
    zon = jnp.concatenate(tiles, axis=0)
    get_mer.wait()
    mer = jnp.concatenate(split2(mer_buf[...]), axis=1)
    mer = jnp.concatenate([mer, mer], axis=0)

    for g in range(count):
        for j in range(4):
            load(g, j).wait()
    for g in range(count):
        for q in range(2):
            t = jnp.dot(zon, buf[g, 192 * q : 192 * q + 192], preferred_element_type=jnp.float32)
            hi, lo = split2(t[:64] + t[64:])
            for i in range(4):
                put = pl.ds(pl.multiple_of(16 * ((4 * q + i + 4 * at_x + at_z) & 7), 16), 16)
                rows = slice(16 * i, 16 * i + 16)
                for j in range(4):
                    lanes = slice(j * ROWS, (j + 1) * ROWS)
                    mid[j, g, put, :ROWS] = hi[rows, lanes]
                    mid[j, g, put, ROWS:] = lo[rows, lanes]
    for j in range(4):
        v = jnp.dot(mid[j].reshape(count * 128, 2 * ROWS), mer, preferred_element_type=jnp.float32)
        for g in range(count):
            u = v[128 * g : 128 * g + 128]
            u = u[:, 128:] + u[:, :128]
            u = u.T.reshape(16, 8, 128)
            lanes = slice(128 * g, 128 * g + 128)
            if along_y:
                stage[j, :, :, lanes] = u
                continue
            for r in range(16):
                stage[j, 4 * (at_z ^ (r % 4)) + (at_x ^ (r // 4)), :, lanes] = u[r]
        store(j).start()
    for j in range(4):
        store(j).wait()


def restrict(x, mer, zon, first, count, along_y):
    lanes = count * 128
    return pl.pallas_call(
        functools.partial(restrict_kernel, first, count, along_y),
        out_shape=[jax.ShapeDtypeStruct((16, 8, lanes), jnp.float32)] * 4,
        in_specs=[ANY] * 3,
        out_specs=[ANY] * 4,
        scratch_shapes=[
            pltpu.VMEM((count, ROWS, 4 * ROWS), jnp.bfloat16),
            pltpu.VMEM((4, count, 128, 2 * ROWS), jnp.bfloat16),
            pltpu.VMEM(mer.shape, jnp.float32),
            pltpu.VMEM(zon.shape, jnp.float32),
            pltpu.VMEM((4, 16, 8, lanes), jnp.float32),
            pltpu.SemaphoreType.DMA((count, 4)),
            pltpu.SemaphoreType.DMA((2,)),
            pltpu.SemaphoreType.DMA((4,)),
        ],
        compiler_params=pltpu.CompilerParams(vmem_limit_bytes=56 * 2**20),
        cost_estimate=pl.CostEstimate(
            flops=count * 800_000_000, bytes_accessed=count * ROWS * ROWS * 16, transcendentals=0
        ),
        name=f"restrict_{first}",
    )(x, mer, zon)


def deal_kernel(p0, p1, p2, p3, near, far, stage, in_sems, out_sems):
    first = lax.axis_index("y") ^ own_member()
    loads = [pltpu.make_async_copy(p, stage.at[k], in_sems.at[k]) for k, p in enumerate((p0, p1, p2, p3))]
    for c in loads:
        c.start()
    for c in loads:
        c.wait()
    for case in range(4):

        @pl.when(first == case)
        def _():
            stores = []
            for k in range(4):
                zlo, core = divmod(case ^ k, 2)
                stores.append(pltpu.make_async_copy(stage.at[k], (near, far)[zlo].at[core], out_sems.at[k]))
            for c in stores:
                c.start()
            for c in stores:
                c.wait()


def deal(parts):
    shape = parts[0].shape
    return pl.pallas_call(
        deal_kernel,
        out_shape=[jax.ShapeDtypeStruct((2, *shape), jnp.float32)] * 2,
        in_specs=[ANY] * 4,
        out_specs=[ANY] * 2,
        scratch_shapes=[
            pltpu.VMEM((4, *shape), jnp.float32),
            pltpu.SemaphoreType.DMA((4,)),
            pltpu.SemaphoreType.DMA((4,)),
        ],
        cost_estimate=pl.CostEstimate(flops=0, bytes_accessed=32 * math.prod(shape), transcendentals=0),
        name="deal",
    )(*parts)


def swap_groups(v):
    group = lax.shift_right_logical(lax.broadcasted_iota(jnp.int32, (8, 128), 1), 4)
    for d in (1, 2, 4):
        moved = (group & d) != 0
        v = [jnp.where(moved, v[(i + d) & 7], v[i]) for i in range(8)]
    return [v[0]] + [pltpu.roll(v[8 - m], 128 - 16 * m, 1) for m in range(1, 8)]


def finish_kernel(levels, tiles1, tiles2, *refs):
    r1, refs = refs[:2], refs[2:]
    r2, out, b1, b2, stage, in_sems, r2_sems, out_sems = refs
    y, me = lax.axis_index("y"), own_member()

    loads = [pltpu.make_async_copy(r1[k], b1.at[k], in_sems.at[k]) for k in range(2)]
    own = 4 * lax.axis_index("x") + lax.axis_index("zhi")

    def load(h, k):
        rows = pl.ds(8 * h, 8)
        return pltpu.make_async_copy(r2.at[k, rows], b2.at[k, rows], r2_sems.at[h, k])

    def store(h, n):
        lanes = pl.ds(128 * h, 128)
        return pltpu.make_async_copy(stage.at[n, :, :, lanes], out.at[levels[n], :, :, lanes], out_sems.at[h, n])

    for c in loads:
        c.start()
    for h in range(2):
        for k in range(4):
            load(h, k).start()
    for c in loads:
        c.wait()
    scale = 1.0 / math.sqrt(M - 1)
    for h in range(2):
        lanes = slice(128 * h, 128 * h + 128)

        def shuffle(k, sums):
            sums = list(sums)
            load(h, k).wait()
            for tile in (*tiles1, *tiles2):
                if tile < CUT:
                    at = 128 * tile
                    p = me ^ k
                    v = [b1[k & 1, own ^ (8 * h + i), k >> 1, :, at : at + 128] for i in range(8)]
                else:
                    at = 128 * (tile - CUT)
                    p = y ^ k
                    v = [b2[k, 8 * h + i, :, at : at + 128] for i in range(8)]
                v = swap_groups(v)
                for i in range(8):
                    level, m = divmod(8 * tile + i, 20)
                    if level in levels:
                        n = level - levels[0]
                        stage[n, p * 20 + m, :, lanes] = v[i]
                        sums[n] = sums[n] + v[i]
            return tuple(sums)

        zero = jnp.zeros((8, 128), jnp.float32)
        sums = lax.fori_loop(0, 4, shuffle, (zero,) * len(levels))
        for n in range(len(levels)):
            mean = sums[n] / M

            def centre(q, _):
                for m in range(20):
                    stage[n, q * 20 + m, :, lanes] = (stage[n, q * 20 + m, :, lanes] - mean) * scale
                return 0

            lax.fori_loop(0, 4, centre, 0)
            store(h, n).start()
    for h in range(2):
        for n in range(len(levels)):
            store(h, n).wait()


def finish(r1, r2):
    levels, tiles1, tiles2 = (0, 1, 2, 3), tuple(range(CUT)), tuple(range(CUT, GROUPS))
    return pl.pallas_call(
        functools.partial(finish_kernel, levels, tiles1, tiles2),
        out_shape=jax.ShapeDtypeStruct((4, M, 8, 256), jnp.float32),
        in_specs=[ANY] * 3,
        out_specs=ANY,
        scratch_shapes=[
            pltpu.VMEM((2, 16, 2, 8, 128 * len(tiles1)), jnp.float32),
            pltpu.VMEM((4, 16, 8, 128 * len(tiles2)), jnp.float32),
            pltpu.VMEM((len(levels), M, 8, 256), jnp.float32),
            pltpu.SemaphoreType.DMA((2,)),
            pltpu.SemaphoreType.DMA((2, 4)),
            pltpu.SemaphoreType.DMA((2, len(levels))),
        ],
        compiler_params=pltpu.CompilerParams(vmem_limit_bytes=16 * 2**20),
        cost_estimate=pl.CostEstimate(
            flops=len(levels) * 2_000_000, bytes_accessed=len(levels) * 1_300_000, transcendentals=0
        ),
        name="finish",
    )(*r1, r2)


def swap(unit, k):
    return [(d, d ^ (unit * k)) for d in range(256)]


def along(unit, parts):
    return [parts[0]] + [lax.ppermute(parts[k], AX, swap(unit, k)) for k in (1, 2, 3)]


def regroup_kernel(*refs):
    parts, outs = refs[:4], refs[4:]
    for i in range(4):
        for k in range(4):
            outs[k][i] = parts[i][:, k]


def regroup(parts):
    lanes = parts[0].shape[-1]
    parts = [p.reshape(4, 4, 8, lanes) for p in parts]
    vmem = pl.BlockSpec(memory_space=pltpu.VMEM)
    return pl.pallas_call(
        regroup_kernel,
        out_shape=[jax.ShapeDtypeStruct((4, 4, 8, lanes), jnp.float32)] * 4,
        in_specs=[vmem] * 4,
        out_specs=[vmem] * 4,
        cost_estimate=pl.CostEstimate(flops=500_000_000_000, bytes_accessed=800_000_000, transcendentals=0),
        name="regroup",
    )(*parts)


def planes():
    return [[(y ^ j) * 64 + y * 16 + b for j in range(4) for b in range(16)] for y in range(4)]


def body(member_predictions, meridional_operator, zonal_operator):
    x = member_predictions.reshape(-1, member_predictions.shape[-1])
    ops = (meridional_operator, zonal_operator)
    one = restrict(x, *ops, 0, CUT, False)
    x, *one = lax.optimization_barrier((x, *one))
    one = along(16, one)
    two = restrict(x, *ops, CUT, GROUPS - CUT, True)
    merged = lax.optimization_barrier((*one, *two))
    one, two = merged[:4], merged[4:]
    near, far = [p.reshape(2, 4, 4, 8, -1) for p in deal(one)]
    far = lax.ppermute(far, AX, swap(128, 1))
    one = along(1, [jnp.stack([near[:, k], far[:, k]], axis=0) for k in range(4)])
    two = jnp.concatenate(along(16, two), axis=0)
    two = lax.all_to_all(two, AX, 0, 0, axis_index_groups=planes(), tiled=True).reshape(4, 16, 8, -1)
    one = along(4, regroup(one))
    one = [p.reshape(4, 2, 2, 8, -1) for p in one]
    stay, leave = [jnp.concatenate([p[:, :, k] for p in one], axis=0) for k in range(2)]
    one = [stay, lax.ppermute(leave, AX, swap(64, 1))]
    return finish(one, two)


def solution(mesh):
    fine = Mesh(mesh.devices.reshape(2, 2, 4, 4, 4), AX)
    member, tile = ("zlo", "core"), ("y", "x", "zhi")
    in_specs = (P(None, member, tile, None), P(), P(tile, None))
    out_specs = P(None, None, tile, member)
    return jax.shard_map(body, mesh=fine, in_specs=in_specs, out_specs=out_specs, check_vma=False)
```

```python
import functools
import math

import jax
import jax.numpy as jnp
from jax import lax
from jax.experimental import pallas as pl
from jax.experimental.pallas import tpu as pltpu
from jax.sharding import Mesh
from jax.sharding import PartitionSpec as P

M = 80
AX = ("zlo", "core", "y", "x", "zhi")
PAIRS = 8
ROWS = 384
CUT, GROUPS = 4, 10
ANY = pl.BlockSpec(memory_space=pl.ANY)


def split2(v):
    hi = v.astype(jnp.bfloat16)
    return hi, (v - hi.astype(jnp.float32)).astype(jnp.bfloat16)


def own_member():
    return 2 * lax.axis_index("zlo") + lax.axis_index("core")


def restrict_kernel(first, count, along_y, x_ref, mer_ref, zon_ref, *rest):
    outs, (buf, mid, mer_buf, zon_buf, stage, in_sems, op_sems, out_sems) = rest[:4], rest[4:]
    base = lax.axis_index("y")
    at_x, at_z = lax.axis_index("x"), lax.axis_index("zhi")

    def load(g):
        return pltpu.make_async_copy(x_ref.at[pl.ds((first + g) * ROWS, ROWS)], buf.at[g], in_sems.at[g])

    def store(j):
        return pltpu.make_async_copy(stage.at[j], outs[j], out_sems.at[j])

    get_mer = pltpu.make_async_copy(mer_ref, mer_buf, op_sems.at[0])
    get_zon = pltpu.make_async_copy(zon_ref, zon_buf, op_sems.at[1])
    get_zon.start()
    get_mer.start()
    for g in range(count):
        load(g).start()
    k = lax.broadcasted_iota(jnp.int32, (48, 192), 0)
    n = lax.broadcasted_iota(jnp.int32, (48, 192), 1)
    spread = jnp.where(lax.rem(n, 48) == k, 1.0, 0.0).astype(jnp.bfloat16)
    row = lax.broadcasted_iota(jnp.int32, (64, 192), 0)
    col = lax.broadcasted_iota(jnp.int32, (64, 192), 1) - 48 * lax.shift_right_logical(row, 4)
    keep = (col >= 0) & (col < 48)
    get_zon.wait()
    tiles = []
    for part in split2(zon_buf[...]):
        wide = jnp.dot(part, spread, preferred_element_type=jnp.float32)
        wide = jnp.concatenate([wide] * 4, axis=0)
        tiles.append(jnp.where(keep, wide, 0.0).astype(jnp.bfloat16))
    zon = jnp.concatenate(tiles, axis=0)
    get_mer.wait()
    mer = jnp.concatenate(split2(mer_buf[...]), axis=1)
    mer = jnp.concatenate([mer, mer], axis=0)

    for g in range(count):
        load(g).wait()
    for g in range(count):
        for q in range(2):
            t = jnp.dot(zon, buf[g, 192 * q : 192 * q + 192], preferred_element_type=jnp.float32)
            hi, lo = split2(t[:64] + t[64:])
            for i in range(4):
                put = pl.ds(pl.multiple_of(16 * ((4 * q + i + 4 * at_x + at_z) & 7), 16), 16)
                rows = slice(16 * i, 16 * i + 16)
                for b in range(4):
                    lanes = slice(b * ROWS, (b + 1) * ROWS)
                    mid[base ^ b, g, put, :ROWS] = hi[rows, lanes]
                    mid[base ^ b, g, put, ROWS:] = lo[rows, lanes]
    for j in range(4):
        v = jnp.dot(mid[j].reshape(count * 128, 2 * ROWS), mer, preferred_element_type=jnp.float32)
        for g in range(count):
            u = v[128 * g : 128 * g + 128]
            u = u[:, 128:] + u[:, :128]
            u = u.T.reshape(16, 8, 128)
            lanes = slice(128 * g, 128 * g + 128)
            if along_y:
                stage[j, :, :, lanes] = u
                continue
            for r in range(16):
                stage[j, 4 * (at_z ^ (r % 4)) + (at_x ^ (r // 4)), :, lanes] = u[r]
        store(j).start()
    for j in range(4):
        store(j).wait()


def restrict(x, mer, zon, first, count, along_y):
    lanes = count * 128
    return pl.pallas_call(
        functools.partial(restrict_kernel, first, count, along_y),
        out_shape=[jax.ShapeDtypeStruct((16, 8, lanes), jnp.float32)] * 4,
        in_specs=[ANY] * 3,
        out_specs=[ANY] * 4,
        scratch_shapes=[
            pltpu.VMEM((count, ROWS, 4 * ROWS), jnp.bfloat16),
            pltpu.VMEM((4, count, 128, 2 * ROWS), jnp.bfloat16),
            pltpu.VMEM(mer.shape, jnp.float32),
            pltpu.VMEM(zon.shape, jnp.float32),
            pltpu.VMEM((4, 16, 8, lanes), jnp.float32),
            pltpu.SemaphoreType.DMA((count,)),
            pltpu.SemaphoreType.DMA((2,)),
            pltpu.SemaphoreType.DMA((4,)),
        ],
        compiler_params=pltpu.CompilerParams(vmem_limit_bytes=56 * 2**20),
        cost_estimate=pl.CostEstimate(
            flops=count * 800_000_000, bytes_accessed=count * ROWS * ROWS * 16, transcendentals=0
        ),
        name=f"restrict_{first}",
    )(x, mer, zon)


def deal_kernel(p0, p1, p2, p3, *rest):
    outs, (stage, in_sems, out_sems) = rest[:8], rest[8:]
    first = lax.axis_index("y") ^ own_member()
    loads = [pltpu.make_async_copy(p, stage.at[k], in_sems.at[k]) for k, p in enumerate((p0, p1, p2, p3))]
    for c in loads:
        c.start()
    for c in loads:
        c.wait()
    for case in range(4):

        @pl.when(first == case)
        def _():
            stores = []
            for k in range(4):
                zlo, core = divmod(case ^ k, 2)
                for z in range(4):
                    to = outs[2 * z + zlo].at[core]
                    stores.append(pltpu.make_async_copy(stage.at[k, pl.ds(4 * z, 4)], to, out_sems.at[k, z]))
            for c in stores:
                c.start()
            for c in stores:
                c.wait()


def deal(parts):
    shape = parts[0].shape
    return pl.pallas_call(
        deal_kernel,
        out_shape=[jax.ShapeDtypeStruct((2, 4, *shape[1:]), jnp.float32)] * 8,
        in_specs=[ANY] * 4,
        out_specs=[ANY] * 8,
        scratch_shapes=[
            pltpu.VMEM((4, *shape), jnp.float32),
            pltpu.SemaphoreType.DMA((4,)),
            pltpu.SemaphoreType.DMA((4, 4)),
        ],
        cost_estimate=pl.CostEstimate(flops=0, bytes_accessed=32 * math.prod(shape), transcendentals=0),
        name="deal",
    )(*parts)


def swap_groups(v):
    group = lax.shift_right_logical(lax.broadcasted_iota(jnp.int32, (8, 128), 1), 4)
    for d in (1, 2, 4):
        moved = (group & d) != 0
        v = [jnp.where(moved, v[(i + d) & 7], v[i]) for i in range(8)]
    return [v[0]] + [pltpu.roll(v[8 - m], 128 - 16 * m, 1) for m in range(1, 8)]


def finish_kernel(levels, tiles1, tiles2, *refs):
    r1, refs = refs[:2], refs[2:]
    r2, out, b1, b2, stage, in_sems, r2_sems, out_sems = refs
    y, me = lax.axis_index("y"), own_member()

    loads = [pltpu.make_async_copy(r1[k], b1.at[k], in_sems.at[k]) for k in range(2)]
    own = 4 * lax.axis_index("x") + lax.axis_index("zhi")

    def load(h, k):
        rows = pl.ds(8 * h, 8)
        return pltpu.make_async_copy(r2.at[k, rows], b2.at[k, rows], r2_sems.at[h, k])

    def store(h, n):
        lanes = pl.ds(128 * h, 128)
        return pltpu.make_async_copy(stage.at[n, :, :, lanes], out.at[levels[n], :, :, lanes], out_sems.at[h, n])

    for c in loads:
        c.start()
    for h in range(2):
        for k in range(4):
            load(h, k).start()
    for c in loads:
        c.wait()
    scale = 1.0 / math.sqrt(M - 1)
    for h in range(2):
        lanes = slice(128 * h, 128 * h + 128)

        def shuffle(k, sums):
            sums = list(sums)
            load(h, k).wait()
            for tile in (*tiles1, *tiles2):
                if tile < CUT:
                    at = 128 * tile
                    p = me ^ k
                    v = [b1[k & 1, own ^ (8 * h + i), k >> 1, :, at : at + 128] for i in range(8)]
                else:
                    at = 128 * (tile - CUT)
                    p = y ^ k
                    v = [b2[k, 8 * h + i, :, at : at + 128] for i in range(8)]
                v = swap_groups(v)
                for i in range(8):
                    level, m = divmod(8 * tile + i, 20)
                    if level in levels:
                        n = level - levels[0]
                        stage[n, p * 20 + m, :, lanes] = v[i]
                        sums[n] = sums[n] + v[i]
            return tuple(sums)

        zero = jnp.zeros((8, 128), jnp.float32)
        sums = lax.fori_loop(0, 4, shuffle, (zero,) * len(levels))
        for n in range(len(levels)):
            mean = sums[n] / M

            def centre(q, _):
                for m in range(20):
                    stage[n, q * 20 + m, :, lanes] = (stage[n, q * 20 + m, :, lanes] - mean) * scale
                return 0

            lax.fori_loop(0, 4, centre, 0)
            store(h, n).start()
    for h in range(2):
        for n in range(len(levels)):
            store(h, n).wait()


def finish(r1, r2):
    levels, tiles1, tiles2 = (0, 1, 2, 3), tuple(range(CUT)), tuple(range(CUT, GROUPS))
    return pl.pallas_call(
        functools.partial(finish_kernel, levels, tiles1, tiles2),
        out_shape=jax.ShapeDtypeStruct((4, M, 8, 256), jnp.float32),
        in_specs=[ANY] * 3,
        out_specs=ANY,
        scratch_shapes=[
            pltpu.VMEM((2, 16, 2, 8, 128 * len(tiles1)), jnp.float32),
            pltpu.VMEM((4, 16, 8, 128 * len(tiles2)), jnp.float32),
            pltpu.VMEM((len(levels), M, 8, 256), jnp.float32),
            pltpu.SemaphoreType.DMA((2,)),
            pltpu.SemaphoreType.DMA((2, 4)),
            pltpu.SemaphoreType.DMA((2, len(levels))),
        ],
        compiler_params=pltpu.CompilerParams(vmem_limit_bytes=16 * 2**20),
        cost_estimate=pl.CostEstimate(
            flops=len(levels) * 2_000_000, bytes_accessed=len(levels) * 1_300_000, transcendentals=0
        ),
        name="finish",
    )(*r1, r2)


def swap(unit, k):
    return [(d, d ^ (unit * k)) for d in range(256)]


def along(unit, parts):
    got = {k: lax.ppermute(parts[k], AX, swap(unit, k)) for k in (2, 1, 3)}
    return [parts[0], got[1], got[2], got[3]]


Z_ORDER = (0, 1, 2, 6, 7, 3, 5, 4)


def regroup_kernel(*refs):
    parts, outs = refs[:8], refs[8:]
    for i, part in zip(Z_ORDER, parts):
        for k in range(4):
            outs[k][i] = part[:, k]


def regroup(parts):
    lanes = parts[0].shape[-1]
    vmem = pl.BlockSpec(memory_space=pltpu.VMEM)
    return pl.pallas_call(
        regroup_kernel,
        out_shape=[jax.ShapeDtypeStruct((8, 2, 8, lanes), jnp.float32)] * 4,
        in_specs=[vmem] * 8,
        out_specs=[vmem] * 4,
        cost_estimate=pl.CostEstimate(flops=500_000_000_000, bytes_accessed=800_000_000, transcendentals=0),
        name="regroup",
    )(*parts)


def planes():
    return [[(y ^ j) * 64 + y * 16 + b for j in range(4) for b in range(16)] for y in range(4)]


def body(member_predictions, meridional_operator, zonal_operator):
    x = member_predictions.reshape(-1, member_predictions.shape[-1])
    ops = (meridional_operator, zonal_operator)
    one = restrict(x, *ops, 0, CUT, False)
    x, *one = lax.optimization_barrier((x, *one))
    one = deal(along(16, one))
    one = [one[i] if i == 0 else lax.ppermute(one[i], AX, swap(1, 128 * (i & 1) + (i >> 1))) for i in Z_ORDER]
    two = restrict(x, *ops, CUT, GROUPS - CUT, True)
    two = jnp.concatenate(along(16, two), axis=0)
    two = lax.all_to_all(two, AX, 0, 0, axis_index_groups=planes(), tiled=True).reshape(4, 16, 8, -1)
    one = along(4, regroup(one))
    stay, leave = [jnp.concatenate([p[:, k] for p in one], axis=0).reshape(16, 2, 8, -1) for k in range(2)]
    one = [stay, lax.ppermute(leave, AX, swap(64, 1))]
    return finish(one, two)


def solution(mesh):
    fine = Mesh(mesh.devices.reshape(2, 2, 4, 4, 4), AX)
    member, tile = ("zlo", "core"), ("y", "x", "zhi")
    in_specs = (P(None, member, tile, None), P(), P(tile, None))
    out_specs = P(None, None, tile, member)
    return jax.shard_map(body, mesh=fine, in_specs=in_specs, out_specs=out_specs, check_vma=False)
```

```python
import functools
import math

import jax
import jax.numpy as jnp
from jax import lax
from jax.experimental import pallas as pl
from jax.experimental.pallas import tpu as pltpu
from jax.sharding import Mesh
from jax.sharding import PartitionSpec as P

M = 80
AX = ("zlo", "core", "y", "x", "zhi")
PAIRS = 8
ROWS = 384
CUT, GROUPS = 4, 10
ANY = pl.BlockSpec(memory_space=pl.ANY)


def split2(v):
    hi = v.astype(jnp.bfloat16)
    return hi, (v - hi.astype(jnp.float32)).astype(jnp.bfloat16)


def own_member():
    return 2 * lax.axis_index("zlo") + lax.axis_index("core")


def restrict_kernel(first, count, along_y, x_ref, mer_ref, zon_ref, *rest):
    outs, (buf, mid, mer_buf, zon_buf, stage, in_sems, op_sems, out_sems) = rest[:4], rest[4:]
    base = lax.axis_index("y")
    at_x, at_z = lax.axis_index("x"), lax.axis_index("zhi")

    def load(g):
        return pltpu.make_async_copy(x_ref.at[pl.ds((first + g) * ROWS, ROWS)], buf.at[g], in_sems.at[g])

    def store(j):
        return pltpu.make_async_copy(stage.at[j], outs[j], out_sems.at[j])

    get_mer = pltpu.make_async_copy(mer_ref, mer_buf, op_sems.at[0])
    get_zon = pltpu.make_async_copy(zon_ref, zon_buf, op_sems.at[1])
    get_zon.start()
    get_mer.start()
    for g in range(count):
        load(g).start()
    k = lax.broadcasted_iota(jnp.int32, (48, 192), 0)
    n = lax.broadcasted_iota(jnp.int32, (48, 192), 1)
    spread = jnp.where(lax.rem(n, 48) == k, 1.0, 0.0).astype(jnp.bfloat16)
    row = lax.broadcasted_iota(jnp.int32, (64, 192), 0)
    col = lax.broadcasted_iota(jnp.int32, (64, 192), 1) - 48 * lax.shift_right_logical(row, 4)
    keep = (col >= 0) & (col < 48)
    get_zon.wait()
    tiles = []
    for part in split2(zon_buf[...]):
        wide = jnp.dot(part, spread, preferred_element_type=jnp.float32)
        wide = jnp.concatenate([wide] * 4, axis=0)
        tiles.append(jnp.where(keep, wide, 0.0).astype(jnp.bfloat16))
    zon = jnp.concatenate(tiles, axis=0)
    get_mer.wait()
    mer = jnp.concatenate(split2(mer_buf[...]), axis=1)
    mer = jnp.concatenate([mer, mer], axis=0)

    for g in range(count):
        load(g).wait()
    for g in range(count):
        for q in range(2):
            t = jnp.dot(zon, buf[g, 192 * q : 192 * q + 192], preferred_element_type=jnp.float32)
            hi, lo = split2(t[:64] + t[64:])
            for i in range(4):
                put = pl.ds(pl.multiple_of(16 * ((4 * q + i + 4 * at_x + at_z) & 7), 16), 16)
                rows = slice(16 * i, 16 * i + 16)
                for b in range(4):
                    lanes = slice(b * ROWS, (b + 1) * ROWS)
                    mid[base ^ b, g, put, :ROWS] = hi[rows, lanes]
                    mid[base ^ b, g, put, ROWS:] = lo[rows, lanes]
    for j in range(4):
        v = jnp.dot(mid[j].reshape(count * 128, 2 * ROWS), mer, preferred_element_type=jnp.float32)
        for g in range(count):
            u = v[128 * g : 128 * g + 128]
            u = u[:, 128:] + u[:, :128]
            u = u.T.reshape(16, 8, 128)
            lanes = slice(128 * g, 128 * g + 128)
            if along_y:
                stage[j, :, :, lanes] = u
                continue
            for r in range(16):
                stage[j, 4 * (at_z ^ (r % 4)) + (at_x ^ (r // 4)), :, lanes] = u[r]
        store(j).start()
    for j in range(4):
        store(j).wait()


def restrict(x, mer, zon, first, count, along_y):
    lanes = count * 128
    return pl.pallas_call(
        functools.partial(restrict_kernel, first, count, along_y),
        out_shape=[jax.ShapeDtypeStruct((16, 8, lanes), jnp.float32)] * 4,
        in_specs=[ANY] * 3,
        out_specs=[ANY] * 4,
        scratch_shapes=[
            pltpu.VMEM((count, ROWS, 4 * ROWS), jnp.bfloat16),
            pltpu.VMEM((4, count, 128, 2 * ROWS), jnp.bfloat16),
            pltpu.VMEM(mer.shape, jnp.float32),
            pltpu.VMEM(zon.shape, jnp.float32),
            pltpu.VMEM((4, 16, 8, lanes), jnp.float32),
            pltpu.SemaphoreType.DMA((count,)),
            pltpu.SemaphoreType.DMA((2,)),
            pltpu.SemaphoreType.DMA((4,)),
        ],
        compiler_params=pltpu.CompilerParams(vmem_limit_bytes=(53 if along_y else 56) * 2**20),
        cost_estimate=pl.CostEstimate(
            flops=count * 800_000_000, bytes_accessed=count * ROWS * ROWS * 16, transcendentals=0
        ),
        name=f"restrict_{first}",
    )(x, mer, zon)


def deal_kernel(p0, p1, p2, p3, *rest):
    outs, (stage, in_sems, out_sems) = rest[:8], rest[8:]
    first = lax.axis_index("y") ^ own_member()
    loads = [pltpu.make_async_copy(p, stage.at[k], in_sems.at[k]) for k, p in enumerate((p0, p1, p2, p3))]
    for c in loads:
        c.start()
    for c in loads:
        c.wait()
    for case in range(4):

        @pl.when(first == case)
        def _():
            stores = []
            for k in range(4):
                zlo, core = divmod(case ^ k, 2)
                for z in range(4):
                    to = outs[2 * z + zlo].at[core]
                    stores.append(pltpu.make_async_copy(stage.at[k, pl.ds(4 * z, 4)], to, out_sems.at[k, z]))
            for c in stores:
                c.start()
            for c in stores:
                c.wait()


def deal(parts):
    shape = parts[0].shape
    return pl.pallas_call(
        deal_kernel,
        out_shape=[jax.ShapeDtypeStruct((2, 4, *shape[1:]), jnp.float32)] * 8,
        in_specs=[ANY] * 4,
        out_specs=[ANY] * 8,
        scratch_shapes=[
            pltpu.VMEM((4, *shape), jnp.float32),
            pltpu.SemaphoreType.DMA((4,)),
            pltpu.SemaphoreType.DMA((4, 4)),
        ],
        cost_estimate=pl.CostEstimate(flops=0, bytes_accessed=32 * math.prod(shape), transcendentals=0),
        name="deal",
    )(*parts)


def swap_groups(v):
    group = lax.shift_right_logical(lax.broadcasted_iota(jnp.int32, (8, 128), 1), 4)
    for d in (1, 2, 4):
        moved = (group & d) != 0
        v = [jnp.where(moved, v[(i + d) & 7], v[i]) for i in range(8)]
    return [v[0]] + [pltpu.roll(v[8 - m], 128 - 16 * m, 1) for m in range(1, 8)]


def finish_kernel(levels, tiles1, tiles2, *refs):
    r1, refs = refs[:2], refs[2:]
    r2, out, b1, b2, stage, in_sems, r2_sems, out_sems = refs
    y, me = lax.axis_index("y"), own_member()

    loads = [pltpu.make_async_copy(r1[k], b1.at[k], in_sems.at[k]) for k in range(2)]
    own = 4 * lax.axis_index("x") + lax.axis_index("zhi")

    def load(h, k):
        rows = pl.ds(8 * h, 8)
        return pltpu.make_async_copy(r2.at[k, rows], b2.at[k, rows], r2_sems.at[h, k])

    def store(h, n):
        lanes = pl.ds(128 * h, 128)
        return pltpu.make_async_copy(stage.at[n, :, :, lanes], out.at[levels[n], :, :, lanes], out_sems.at[h, n])

    for c in loads:
        c.start()
    for h in range(2):
        for k in range(4):
            load(h, k).start()
    for c in loads:
        c.wait()
    scale = 1.0 / math.sqrt(M - 1)
    for h in range(2):
        lanes = slice(128 * h, 128 * h + 128)

        def shuffle(k, sums):
            sums = list(sums)
            load(h, k).wait()
            for tile in (*tiles1, *tiles2):
                if tile < CUT:
                    at = 128 * tile
                    p = me ^ k
                    v = [b1[k & 1, own ^ (8 * h + i), k >> 1, :, at : at + 128] for i in range(8)]
                else:
                    at = 128 * (tile - CUT)
                    p = y ^ k
                    v = [b2[k, 8 * h + i, :, at : at + 128] for i in range(8)]
                v = swap_groups(v)
                for i in range(8):
                    level, m = divmod(8 * tile + i, 20)
                    if level in levels:
                        n = level - levels[0]
                        stage[n, p * 20 + m, :, lanes] = v[i]
                        sums[n] = sums[n] + v[i]
            return tuple(sums)

        zero = jnp.zeros((8, 128), jnp.float32)
        sums = lax.fori_loop(0, 4, shuffle, (zero,) * len(levels))
        for n in range(len(levels)):
            mean = sums[n] / M

            def centre(q, _):
                for m in range(20):
                    stage[n, q * 20 + m, :, lanes] = (stage[n, q * 20 + m, :, lanes] - mean) * scale
                return 0

            lax.fori_loop(0, 4, centre, 0)
            store(h, n).start()
    for h in range(2):
        for n in range(len(levels)):
            store(h, n).wait()


def finish(r1, r2):
    levels, tiles1, tiles2 = (0, 1, 2, 3), tuple(range(CUT)), tuple(range(CUT, GROUPS))
    return pl.pallas_call(
        functools.partial(finish_kernel, levels, tiles1, tiles2),
        out_shape=jax.ShapeDtypeStruct((4, M, 8, 256), jnp.float32),
        in_specs=[ANY] * 3,
        out_specs=ANY,
        scratch_shapes=[
            pltpu.VMEM((2, 16, 2, 8, 128 * len(tiles1)), jnp.float32),
            pltpu.VMEM((4, 16, 8, 128 * len(tiles2)), jnp.float32),
            pltpu.VMEM((len(levels), M, 8, 256), jnp.float32),
            pltpu.SemaphoreType.DMA((2,)),
            pltpu.SemaphoreType.DMA((2, 4)),
            pltpu.SemaphoreType.DMA((2, len(levels))),
        ],
        compiler_params=pltpu.CompilerParams(vmem_limit_bytes=16 * 2**20),
        cost_estimate=pl.CostEstimate(
            flops=len(levels) * 2_000_000, bytes_accessed=len(levels) * 1_300_000, transcendentals=0
        ),
        name="finish",
    )(*r1, r2)


def swap(unit, k):
    return [(d, d ^ (unit * k)) for d in range(256)]


def along(unit, parts):
    got = {k: lax.ppermute(parts[k], AX, swap(unit, k)) for k in (2, 1, 3)}
    return [parts[0], got[1], got[2], got[3]]


Z_ORDER = (0, 1, 2, 6, 7, 3, 5, 4)


def regroup_kernel(*refs):
    parts, outs = refs[:8], refs[8:]
    for i, part in zip(Z_ORDER, parts):
        for k in range(4):
            outs[k][i] = part[:, k]


def regroup(parts):
    lanes = parts[0].shape[-1]
    vmem = pl.BlockSpec(memory_space=pltpu.VMEM)
    return pl.pallas_call(
        regroup_kernel,
        out_shape=[jax.ShapeDtypeStruct((8, 2, 8, lanes), jnp.float32)] * 4,
        in_specs=[vmem] * 8,
        out_specs=[vmem] * 4,
        cost_estimate=pl.CostEstimate(flops=500_000_000_000, bytes_accessed=800_000_000, transcendentals=0),
        name="regroup",
    )(*parts)


def planes():
    return [[(y ^ j) * 64 + y * 16 + b for j in range(4) for b in range(16)] for y in range(4)]


def body(member_predictions, meridional_operator, zonal_operator):
    x = member_predictions.reshape(-1, member_predictions.shape[-1])
    ops = (meridional_operator, zonal_operator)
    one = restrict(x, *ops, 0, CUT, False)
    x, *one = lax.optimization_barrier((x, *one))
    one = deal(along(16, one))
    one = [one[i] if i == 0 else lax.ppermute(one[i], AX, swap(1, 128 * (i & 1) + (i >> 1))) for i in Z_ORDER]
    two = restrict(x, *ops, CUT, GROUPS - CUT, True)
    two = jnp.concatenate(along(16, two), axis=0)
    two = lax.all_to_all(two, AX, 0, 0, axis_index_groups=planes(), tiled=True).reshape(4, 16, 8, -1)
    one = along(4, regroup(one))
    stay, leave = [jnp.concatenate([p[:, k] for p in one], axis=0).reshape(16, 2, 8, -1) for k in range(2)]
    one = [stay, lax.ppermute(leave, AX, swap(64, 1))]
    return finish(one, two)


def solution(mesh):
    fine = Mesh(mesh.devices.reshape(2, 2, 4, 4, 4), AX)
    member, tile = ("zlo", "core"), ("y", "x", "zhi")
    in_specs = (P(None, member, tile, None), P(), P(tile, None))
    out_specs = P(None, None, tile, member)
    return jax.shard_map(body, mesh=fine, in_specs=in_specs, out_specs=out_specs, check_vma=False)
```
